32 devices in a mesh: dp: 8 (over z, y), row: 2 (over core), col: 2 (over x).
Axes of the slice: x: 2, y: 2, z: 4, core: 2. Of those that a mesh axis runs over, the one named last changes fastest.
Arguments:
- block_input: bfloat16 [4096, 2560], P(('dp', 'col')), may hold values from -6 to 6
- cotangent: bfloat16 [4096, 2560], P(('dp', 'col'), 'row'), may hold values from -6 to 6
- seq_lengths: int32 [32], replicated, may hold values from 16 to 128, as said below
- seq_owner: int32 [32], replicated, may hold values from 0 to 15, as said below
- norm_gain: bfloat16 [2560], P('row'), may hold values from 0.5 to 1.5
- proj_zx: bfloat16 [2560, 2, 5120], P('row', None, 'col'), may hold values from -0.125 to 0.125
- proj_bc: bfloat16 [2560, 256], P('row'), may hold values from -0.125 to 0.125
- proj_dt: bfloat16 [2560, 80], P('row', 'col'), may hold values from -0.125 to 0.125
- proj_out: bfloat16 [5120, 2560], P('col', 'row'), may hold values from -0.078125 to 0.078125
- inner_kernel: float32 [4, 5120], P(None, 'col'), may hold values from -3 to 3
- inner_offset: float32 [5120], P('col'), may hold values from -1.5 to 1.5
- shared_kernel: float32 [4, 256], replicated, may hold values from -3 to 3
- shared_offset: float32 [256], replicated, may hold values from -1.5 to 1.5
- decay_log: float32 [80], P('col'), may hold values from 0 to 2.77
- step_bias: float32 [80], P('col'), may hold values from -6 to -2
- skip_gain: float32 [80], P('col'), may hold values from 0.5 to 1.5
- output_gain: bfloat16 [5120], P('col'), may hold values from 0.5 to 1.5
Outputs:
- block_output: bfloat16 [4096, 2560], P(('dp', 'col'), 'row')
- input_grad: float32 [4096, 2560], P(('dp', 'col'), 'row')
- grad_norm: float32 [2560], P('row')
- grad_inproj: float32 [2560, 2, 5120], P('row', None, 'col')
- grad_shared: float32 [2560, 256], P('row')
- grad_steps: float32 [2560, 80], P('row', 'col')
- grad_outproj: float32 [5120, 2560], P('col', 'row')
- grad_kernel: float32 [4, 5120], P(None, 'col')
- grad_offset: float32 [5120], P('col')
- grad_skernel: float32 [4, 256], replicated
- grad_soffset: float32 [256], replicated
- grad_decay: float32 [80], P('col')
- grad_stepbias: float32 [80], P('col')
- grad_skip: float32 [80], P('col')
- grad_ogain: float32 [5120], P('col')
The draws below stay inside these ranges and needn't reach their ends.
Inputs may be any that keep to these rules, and one draw needn't show every extreme that they name: `seq_lengths`: the lengths of the 2 sequences of one bucket sum to at most 256; in every draw some bucket holds 2 sequences of exactly 128 rows, so that its sum is 256. `seq_owner`: every bucket owns exactly 2 sequences.
All inputs are finite; a program needn't handle non-finite values.
Results may differ from the reference program's by a relative error of at most 0.0079.
The reference program's roundings to bfloat16 on the way count: a program that leaves them out, or rounds other values in their place, can miss the bound.
Values may be sent and summed in bfloat16 or wider, within the bound.
A program may use at most 256 MiB of HBM per device.

```python
import jax
import jax.numpy as jnp
from jax import lax

D = 2560
DI = 5120
H = 80
P_SIZE = 64
N = 128
K = 4
CAP = 256
SPB = 2
BUCKETS = 16
NSEQ = 32
TOKENS = 4096
DIC = 2560
HL = 40
N_COL = 2


def packing(key):
    folded = jax.random.fold_in(key, 11)
    key_perm, key_raw, key_full = jax.random.split(folded, 3)
    slot_of = jax.random.permutation(key_perm, NSEQ)
    longest = CAP // SPB
    lengths = jax.random.randint(key_raw, (BUCKETS, SPB), CAP // (8 * SPB), longest + 1)
    chosen = jax.random.randint(key_full, (), 0, BUCKETS)
    lengths = jnp.where((jnp.arange(BUCKETS) == chosen)[:, None], longest, lengths)
    lengths = lengths.reshape(NSEQ)
    return (lengths[slot_of].astype(jnp.int32), (slot_of // SPB).astype(jnp.int32))


def draw_seq_lengths(key, part):
    return packing(key)[0]


def draw_seq_owner(key, part):
    return packing(key)[1]


def block_levels(own_key, dims, shards, smallest, top_value):
    level = 1.0
    for axis_at, blocks in shards:
        heights = jax.random.uniform(jax.random.fold_in(jax.random.fold_in(own_key, 6), axis_at), (blocks,), jnp.float32, smallest / len(shards), top_value / len(shards))
        level = level * jnp.repeat(jnp.exp(heights), dims[axis_at] // blocks).reshape((-1,) + (1,) * (len(dims) - 1 - axis_at))
    return level


def scatter_about(key, shape, scale, bound, cuts=(), kind=jnp.bfloat16):
    array = jax.random.normal(key, shape, jnp.float32) * scale
    if len(cuts) > 0:
        array = block_levels(key, shape, cuts, -0.22, 0.18) * array
    return jnp.clip(array, min=-bound, max=bound).astype(kind)


def setup_inputs(seed: int = 0) -> dict:
    splits = jax.random.split(jax.random.key(seed), 18)
    return {
        "block_input": scatter_about(splits[0], (TOKENS, D), 1.0, 6.0, ((0, 16),)),
        "cotangent": scatter_about(splits[1], (TOKENS, D), 1.0, 6.0, ((0, 16), (1, 2))),
        "seq_lengths": draw_seq_lengths(jax.random.fold_in(splits[17], 71), 0),
        "seq_owner": draw_seq_owner(jax.random.fold_in(splits[17], 71), 0),
        "norm_gain": jnp.clip(1.0 + 0.1 * jax.random.normal(splits[4], (D,), jnp.float32), 0.5, 1.5).astype(jnp.bfloat16),
        "proj_zx": scatter_about(splits[5], (D, 2, DI), D ** -0.5, 0.125, ((0, 2), (2, 2))),
        "proj_bc": scatter_about(splits[6], (D, 2 * N), D ** -0.5, 0.125, ((0, 2),)),
        "proj_dt": scatter_about(splits[7], (D, H), D ** -0.5, 0.125, ((0, 2), (1, 2))),
        "proj_out": scatter_about(splits[8], (DI, D), DI ** -0.5, 0.078125, ((0, 2), (1, 2))),
        "inner_kernel": scatter_about(splits[9], (K, DI), K ** -0.5, 3.0, ((1, 2),), jnp.float32),
        "inner_offset": scatter_about(splits[10], (DI,), 0.3, 1.5, ((0, 2),), jnp.float32),
        "shared_kernel": scatter_about(splits[11], (K, 2 * N), K ** -0.5, 3.0, (), jnp.float32),
        "shared_offset": scatter_about(splits[12], (2 * N,), 0.3, 1.5, (), jnp.float32),
        "decay_log": jnp.clip(2.77 * jax.random.uniform(splits[13], (H,), jnp.float32) ** block_levels(splits[13], (H,), ((0, 2),), -0.2, 0.2), 0.0, 2.77),
        "step_bias": jnp.clip(-6.0 + 4.0 * jax.random.uniform(splits[14], (H,), jnp.float32) ** block_levels(splits[14], (H,), ((0, 2),), -0.2, 0.2), -6.0, -2.0),
        "skip_gain": jnp.clip(0.5 + 1.0 * jax.random.uniform(splits[15], (H,), jnp.float32) ** block_levels(splits[15], (H,), ((0, 2),), -0.2, 0.2), 0.5, 1.5),
        "output_gain": jnp.clip(1.0 + 0.1 * jax.random.normal(splits[16], (DI,), jnp.float32), 0.5, 1.5).astype(jnp.bfloat16),
    }


@jax.custom_vjp
def low(v):
    return lax.optimization_barrier(v.astype(jnp.bfloat16)).astype(jnp.float32)

@jax.custom_vjp
def low_back(v):
    return v

def low_keep(v):
    return (low(v), None)

def low_pass(kept, grad):
    return (grad,)

def back_keep(v):
    return (v, None)

def back_low(kept, grad):
    return (low(grad),)
low.defvjp(low_keep, low_pass)
low_back.defvjp(back_keep, back_low)
EPSILON = 1e-05
PRECISE = lax.Precision.HIGHEST

def layout(seq_lengths, seq_owner, bucket):
    owned = seq_owner == bucket
    owned_len = jnp.where(owned, seq_lengths, 0).astype(jnp.int32)
    starts = (jnp.cumsum(owned_len) - owned_len).astype(jnp.int32)
    places = jnp.arange(CAP, dtype=jnp.int32)[:, None]
    ends = (starts + seq_lengths).astype(jnp.int32)
    inside = owned[None, :] & (places >= starts[None, :]) & (places < ends[None, :])
    live_rows = jnp.any(inside, axis=1)
    seq_index = jnp.arange(seq_lengths.shape[0], dtype=jnp.int32)
    seq_ids = lax.optimization_barrier(jnp.sum(jnp.where(inside, seq_index[None, :], 0), axis=1)).astype(jnp.int32)
    seq_ids = jnp.where(live_rows, seq_ids, -1).astype(jnp.int32)
    return (seq_ids, live_rows.astype(jnp.float32))

def convolve(channels, kernel, offset, seq_ids, live_rows):
    tap_count = kernel.shape[0]
    summed_in = offset[None, :] + kernel[tap_count - 1][None, :] * channels
    for lag_steps in range(1, tap_count):
        lagged = jnp.concatenate([jnp.zeros((lag_steps, channels.shape[1]), jnp.float32), channels[:-lag_steps]], axis=0)
        prior_ids = jnp.concatenate([jnp.full((lag_steps,), -1, jnp.int32), seq_ids[:-lag_steps]])
        same_seq = jnp.where((prior_ids == seq_ids) & (live_rows > 0), 1.0, 0.0).astype(jnp.float32)
        summed_in = summed_in + kernel[tap_count - 1 - lag_steps][None, :] * lagged * same_seq[:, None]
    return summed_in

def bucket_block(rows_in, seq_ids, live_rows, params):
    norm_gain, proj_zx, proj_bc, proj_dt, proj_out, inner_kernel, inner_offset, shared_kernel, shared_offset, decay_log, step_bias, skip_gain, output_gain = params
    rscale = lax.rsqrt(lax.optimization_barrier(jnp.mean(rows_in * rows_in, axis=1, keepdims=True)) + EPSILON)
    normed = low(rows_in * rscale * norm_gain[None, :])
    gate_all = low_back(jnp.dot(normed, proj_zx[:, 0, :], precision=PRECISE))
    inner_all = low_back(jnp.dot(normed, proj_zx[:, 1, :], precision=PRECISE))
    step_all = low_back(jnp.dot(normed, proj_dt, precision=PRECISE))
    shared_all = jnp.dot(normed, proj_bc, precision=PRECISE)
    lower = jnp.arange(CAP)[:, None] >= jnp.arange(CAP)[None, :]
    live_pairs = (seq_ids[:, None] == seq_ids[None, :]) & (live_rows[:, None] > 0) & (live_rows[None, :] > 0) & lower
    pair_mask = live_pairs.astype(jnp.float32)
    pieces = []
    for group_index in range(N_COL):
        head_lo = group_index * HL
        chan_lo = group_index * DIC
        shared_copy = low_back(shared_all)
        mixed_x = jax.nn.silu(convolve(inner_all[:, chan_lo:chan_lo + DIC], inner_kernel[:, chan_lo:chan_lo + DIC], inner_offset[chan_lo:chan_lo + DIC], seq_ids, live_rows))
        mixed_bc = jax.nn.silu(convolve(shared_copy, shared_kernel, shared_offset, seq_ids, live_rows))
        inputs_b = mixed_bc[:, :N]
        inputs_c = mixed_bc[:, N:]
        step_sizes = jax.nn.softplus(step_all[:, head_lo:head_lo + HL] + step_bias[head_lo:head_lo + HL][None, :])
        decay_rate = step_sizes * (-jnp.exp(decay_log[head_lo:head_lo + HL]))[None, :]
        cumulated = jnp.cumsum(decay_rate, axis=0)
        scores = jnp.dot(inputs_c, inputs_b.T, precision=PRECISE)
        values = mixed_x.reshape(CAP, HL, P_SIZE)

        def one_head(head_item):
            cum_head, step_head, value_head, skip_head = head_item
            gap = jnp.where(live_pairs, cum_head[:, None] - cum_head[None, :], 0.0)
            weights = jnp.exp(gap) * pair_mask * scores * step_head[None, :]
            return jnp.dot(weights, value_head, precision=PRECISE) + skip_head * value_head
        head_out = lax.map(jax.checkpoint(one_head), (cumulated.T, step_sizes.T, values.transpose(1, 0, 2), skip_gain[head_lo:head_lo + HL]))
        ssm_out = head_out.transpose(1, 0, 2).reshape(CAP, DIC) * live_rows[:, None]
        pieces.append(ssm_out * jax.nn.silu(gate_all[:, chan_lo:chan_lo + DIC]))
    gated_rows = jnp.concatenate(pieces, axis=1)
    onorm = lax.rsqrt(lax.optimization_barrier(jnp.mean(gated_rows * gated_rows, axis=1, keepdims=True)) + EPSILON)
    branch = low(gated_rows * onorm * output_gain[None, :])
    return jnp.dot(branch, proj_out, precision=PRECISE)

def reference(block_input, cotangent, seq_lengths, seq_owner, norm_gain, proj_zx, proj_bc, proj_dt, proj_out, inner_kernel, inner_offset, shared_kernel, shared_offset, decay_log, step_bias, skip_gain, output_gain):
    bucket_ids = jnp.arange(BUCKETS, dtype=jnp.int32)
    all_ids, all_live = jax.vmap(lambda which: layout(seq_lengths, seq_owner, which))(bucket_ids)
    floats = tuple((item.astype(jnp.float32) for item in (block_input, norm_gain, proj_zx, proj_bc, proj_dt, proj_out, inner_kernel, inner_offset, shared_kernel, shared_offset, decay_log, step_bias, skip_gain, output_gain)))

    def forward(inputs, *params):

        def visit(carried_in, block_item):
            rows_in, ids_in, live_in = block_item
            return (carried_in, jax.checkpoint(bucket_block)(rows_in, ids_in, live_in, params))
        _, branch_rows = lax.scan(visit, jnp.zeros((), jnp.float32), (inputs.reshape(BUCKETS, CAP, D), all_ids, all_live))
        return inputs + branch_rows.reshape(TOKENS, D)
    result, pull_back = jax.vjp(forward, *floats)
    grads = pull_back(cotangent.astype(jnp.float32))
    return (result.astype(jnp.bfloat16), grads[0], grads[1], grads[2], grads[3], grads[4], grads[5], grads[6], grads[7], grads[8], grads[9], grads[10], grads[11], grads[12], grads[13])
```

```python
import jax
import jax.numpy as jnp
from jax import lax
from jax.sharding import PartitionSpec as P

D = 2560
DI = 5120
CAP = 256


EPSILON = 1e-05
PRECISE = lax.Precision.HIGHEST


def layout(seq_lengths, seq_owner, bucket, capacity):
    owned = seq_owner == bucket
    owned_len = jnp.where(owned, seq_lengths, 0)
    order = jnp.arange(seq_lengths.shape[0], dtype=jnp.int32)
    starts = jnp.sum(jnp.where(order[None, :] < order[:, None], owned_len[None, :], 0), axis=1)
    places = jnp.arange(capacity, dtype=jnp.int32)[:, None]
    ends = starts + seq_lengths
    inside = owned[None, :] & (places >= starts[None, :]) & (places < ends[None, :])
    live_rows = jnp.any(inside, axis=1)
    seq_index = jnp.arange(seq_lengths.shape[0], dtype=jnp.int32)
    seq_ids = jnp.sum(jnp.where(inside, seq_index[None, :], 0), axis=1)
    seq_ids = jnp.where(live_rows, seq_ids, -1)
    return (seq_ids, live_rows.astype(jnp.float32))


def convolve(channels, kernel, offset, seq_ids, live_rows):
    tap_count = kernel.shape[0]
    summed_in = offset[None, :] + kernel[tap_count - 1][None, :] * channels
    for lag_steps in range(1, tap_count):
        lagged = jnp.concatenate(
            [jnp.zeros((lag_steps, channels.shape[1]), jnp.float32), channels[:-lag_steps]], axis=0
        )
        prior_ids = jnp.concatenate([jnp.full((lag_steps,), -1, jnp.int32), seq_ids[:-lag_steps]])
        same_seq = jnp.where((prior_ids == seq_ids) & (live_rows > 0), 1.0, 0.0).astype(jnp.float32)
        summed_in = (
            summed_in + kernel[tap_count - 1 - lag_steps][None, :] * lagged * same_seq[:, None]
        )
    return summed_in


def mix_bucket(values, bmat, cmat, sizes, rates, skip_gain, ids, live):
    rows_all, head_count, head_dim = values.shape
    lower = jnp.arange(rows_all)[:, None] >= jnp.arange(rows_all)[None, :]
    cumulated = jnp.dot(lower.astype(jnp.float32), rates, precision=PRECISE)
    pair_live = (
        (ids[:, None] == ids[None, :]) & (live[:, None] > 0) & (live[None, :] > 0) & lower
    )
    scores = jnp.dot(cmat, bmat.T, precision=PRECISE)
    gap = jnp.where(pair_live[:, :, None], cumulated[:, None, :] - cumulated[None, :, :], 0.0)
    weights = (
        jnp.exp(gap) * (pair_live.astype(jnp.float32) * scores)[:, :, None] * sizes[None, :, :]
    )
    within = jnp.einsum("tsh,shp->thp", weights, values, precision=PRECISE)
    mixed_out = (within + skip_gain[None, :, None] * values) * live[:, None, None]
    return mixed_out.reshape(rows_all, head_count * head_dim)


def sum_rows_over_dp(part, shared_cols=0):
    piece = lax.psum_scatter(
        part.astype(jnp.bfloat16), "dp", scatter_dimension=0, tiled=True
    )
    if shared_cols:
        own = piece.shape[1] - shared_cols
        tail = lax.psum(piece[:, own:].astype(jnp.float32), "col").astype(jnp.bfloat16)
        piece = jnp.concatenate([piece[:, :own], tail], axis=1)
    return lax.all_gather(piece, "dp", axis=0, tiled=True)


def mixer_local(
    conv_in,
    narrow_in,
    inner_kernel,
    inner_offset,
    shared_kernel,
    shared_offset,
    decay_log,
    step_bias,
    skip_gain,
    seq_ids,
    live_rows,
):
    inner_size = inner_kernel.shape[1]
    state_size = shared_kernel.shape[1] // 2
    head_count = decay_log.shape[0]
    shared_in = narrow_in[:, : 2 * state_size]
    step_raw = narrow_in[:, 2 * state_size :]
    mixed_x = jax.nn.silu(convolve(conv_in, inner_kernel, inner_offset, seq_ids, live_rows))
    mixed_bc = jax.nn.silu(convolve(shared_in, shared_kernel, shared_offset, seq_ids, live_rows))
    step_sizes = jax.nn.softplus(step_raw + step_bias[None, :])
    decay_rate = step_sizes * (-jnp.exp(decay_log))[None, :]
    values = mixed_x.reshape(mixed_x.shape[0], head_count, inner_size // head_count)
    return mix_bucket(
        values,
        mixed_bc[:, :state_size],
        mixed_bc[:, state_size:],
        step_sizes,
        decay_rate,
        skip_gain,
        seq_ids,
        live_rows,
    )


def per_device(
    block_input,
    cotangent,
    seq_lengths,
    seq_owner,
    norm_gain,
    proj_zx,
    proj_bc,
    proj_dt,
    proj_out,
    inner_kernel,
    inner_offset,
    shared_kernel,
    shared_offset,
    decay_log,
    step_bias,
    skip_gain,
    output_gain,
):
    row_count = lax.axis_size("row")
    col_count = lax.axis_size("col")
    row_index = lax.axis_index("row")
    col_index = lax.axis_index("col")
    data_index = lax.axis_index("dp")
    width_part = norm_gain.shape[0]
    inner_size = proj_zx.shape[2]
    state_size = proj_bc.shape[1] // 2
    tap_count = inner_kernel.shape[0]
    capacity = CAP
    bucket = data_index * row_count + row_index
    seq_ids, live_rows = layout(seq_lengths, seq_owner, bucket, capacity)
    rscale = lax.rsqrt(
        jnp.mean(jnp.square(block_input.astype(jnp.float32)), axis=1, keepdims=True) + EPSILON
    )
    own_cols = lax.dynamic_slice_in_dim(block_input, row_index * width_part, width_part, 1).astype(
        jnp.float32
    )
    normalized = own_cols * rscale
    gain_f = norm_gain.astype(jnp.float32)
    normed = (normalized * gain_f[None, :]).astype(jnp.bfloat16)
    normed_all = lax.all_gather(normed, "col", axis=0, tiled=True)
    weight_zx = proj_zx.reshape(width_part, 2 * inner_size)
    weight_narrow = jnp.concatenate([proj_bc, proj_dt], axis=1)
    zx_in = lax.psum_scatter(
        jnp.dot(normed_all, weight_zx, preferred_element_type=jnp.float32),
        "row",
        scatter_dimension=0,
        tiled=True,
    )
    narrow_in = lax.psum_scatter(
        jnp.dot(normed_all, weight_narrow, preferred_element_type=jnp.float32),
        "row",
        scatter_dimension=0,
        tiled=True,
    )
    gate_in = zx_in[:, :inner_size]
    conv_in = zx_in[:, inner_size:]

    def local_piece(*operands):
        return mixer_local(*operands, seq_ids, live_rows)

    ssm_rows, pull_back = jax.vjp(
        local_piece,
        conv_in,
        narrow_in,
        inner_kernel,
        inner_offset,
        shared_kernel,
        shared_offset,
        decay_log,
        step_bias,
        skip_gain,
    )
    gated_rows, gate_back = jax.vjp(
        lambda ssm_value, gate_value: ssm_value * jax.nn.silu(gate_value), ssm_rows, gate_in
    )
    square_sum = lax.psum(jnp.sum(gated_rows * gated_rows, axis=1), "col")
    rnorm = lax.rsqrt(square_sum / DI + EPSILON)[:, None]
    out_gain = output_gain.astype(jnp.float32)
    branch = (gated_rows * rnorm * out_gain[None, :]).astype(jnp.bfloat16)
    branch_all = lax.all_gather(branch, "row", axis=0, tiled=True)
    row_piece = branch_all
    branch_out = lax.psum_scatter(
        jnp.dot(row_piece, proj_out, preferred_element_type=jnp.float32),
        "col",
        scatter_dimension=0,
        tiled=True,
    )
    block_output = (own_cols + branch_out).astype(jnp.bfloat16)
    cot_all = lax.all_gather(cotangent, "col", axis=0, tiled=True)
    row_piece = cot_all
    branch_grad = lax.psum_scatter(
        lax.dot_general(
            row_piece, proj_out, (((1,), (1,)), ((), ())), preferred_element_type=jnp.float32
        ),
        "row",
        scatter_dimension=0,
        tiled=True,
    )
    outproj_part = lax.dot_general(
        branch_all, cot_all, (((0,), (0,)), ((), ())), preferred_element_type=jnp.float32
    )
    outproj_total = sum_rows_over_dp(outproj_part).astype(jnp.float32)
    scaled_grad = branch_grad * out_gain[None, :]
    cross_sum = lax.psum(jnp.sum(scaled_grad * gated_rows, axis=1), "col")
    gated_grad = rnorm * scaled_grad - gated_rows * rnorm**3 * (cross_sum / DI)[:, None]
    ogain_part = jnp.sum(branch_grad * gated_rows * rnorm, axis=0)
    ssm_grad, gate_grad = gate_back(gated_grad)
    gate_all = lax.all_gather(gate_grad.astype(jnp.bfloat16), "row", axis=0, tiled=True)
    gate_total = sum_rows_over_dp(
        lax.dot_general(
            normed_all, gate_all, (((0,), (0,)), ((), ())), preferred_element_type=jnp.float32
        )
    )
    local_grads = pull_back(ssm_grad)
    inner_all = lax.all_gather(
        local_grads[0].astype(jnp.bfloat16), "row", axis=0, tiled=True
    )
    narrow_all = lax.all_gather(
        local_grads[1].astype(jnp.bfloat16), "row", axis=0, tiled=True
    )
    normed_grad = lax.psum_scatter(
        lax.dot_general(
            jnp.concatenate([gate_all, inner_all], axis=1),
            weight_zx,
            (((1,), (1,)), ((), ())),
            preferred_element_type=jnp.float32,
        )
        + lax.dot_general(
            narrow_all, weight_narrow, (((1,), (1,)), ((), ())), preferred_element_type=jnp.float32
        ),
        "col",
        scatter_dimension=0,
        tiled=True,
    )
    inner_total = sum_rows_over_dp(
        lax.dot_general(
            normed_all, inner_all, (((0,), (0,)), ((), ())), preferred_element_type=jnp.float32
        )
    )
    narrow_part = lax.dot_general(
        normed_all, narrow_all, (((0,), (0,)), ((), ())), preferred_element_type=jnp.float32
    )
    narrow_total = sum_rows_over_dp(
        jnp.concatenate([narrow_part[:, 2 * state_size :], narrow_part[:, : 2 * state_size]], 1),
        2 * state_size,
    ).astype(jnp.float32)
    head_count = decay_log.shape[0]
    steps_total = narrow_total[:, :head_count]
    shared_total = narrow_total[:, head_count:]
    inproj_total = jnp.stack([gate_total, inner_total], axis=1).astype(jnp.float32)
    scaled_in = normed_grad * gain_f[None, :]
    norm_part = jnp.sum(normed_grad * normalized, axis=0)
    row_stat = lax.psum(jnp.sum(scaled_in * normalized, axis=1), "row")
    input_grad = cotangent.astype(jnp.float32) + rscale * (
        scaled_in - normalized * (row_stat / D)[:, None]
    )
    row_hot = (jnp.arange(row_count) == row_index).astype(jnp.float32)
    col_hot = (jnp.arange(col_count) == col_index).astype(jnp.float32)
    gain_slot = row_hot[:, None] * norm_part[None, :]
    head_stack = jnp.stack([local_grads[6], local_grads[7], local_grads[8]], axis=0)
    head_slot = col_hot[None, :, None] * head_stack[:, None, :]
    chan_stack = jnp.concatenate(
        [local_grads[2], local_grads[3][None, :], ogain_part[None, :]], axis=0
    )
    chan_slot = col_hot[None, :, None] * chan_stack[:, None, :]
    shared_stack = jnp.concatenate([local_grads[4], local_grads[5][None, :]], axis=0)
    summed = lax.psum(
        (gain_slot, head_slot, chan_slot, shared_stack), ("dp", "row", "col")
    )
    gain_total = lax.dynamic_index_in_dim(summed[0], row_index, 0, keepdims=False)
    head_total = lax.dynamic_index_in_dim(summed[1], col_index, 1, keepdims=False)
    chan_total = lax.dynamic_index_in_dim(summed[2], col_index, 1, keepdims=False)
    stack_total = summed[3]
    return (
        block_output,
        input_grad,
        gain_total,
        inproj_total,
        shared_total,
        steps_total,
        outproj_total,
        chan_total[:tap_count],
        chan_total[tap_count],
        stack_total[:tap_count],
        stack_total[tap_count],
        head_total[0],
        head_total[1],
        head_total[2],
        chan_total[tap_count + 1],
    )


def solution(mesh):
    return jax.shard_map(
        per_device,
        mesh=mesh,
        in_specs=(
            P(("dp", "col"), None),
            P(("dp", "col"), "row"),
            P(),
            P(),
            P("row"),
            P("row", None, "col"),
            P("row", None),
            P("row", "col"),
            P("col", "row"),
            P(None, "col"),
            P("col"),
            P(),
            P(),
            P("col"),
            P("col"),
            P("col"),
            P("col"),
        ),
        out_specs=(
            P(("dp", "col"), "row"),
            P(("dp", "col"), "row"),
            P("row"),
            P("row", None, "col"),
            P("row", None),
            P("row", "col"),
            P("col", "row"),
            P(None, "col"),
            P("col"),
            P(),
            P(),
            P("col"),
            P("col"),
            P("col"),
            P("col"),
        ),
        check_vma=False,
    )
```

```python
import jax
import jax.numpy as jnp
from jax import lax
from jax.sharding import PartitionSpec as P

D = 2560
DI = 5120
CAP = 256


EPSILON = 1e-05
PRECISE = lax.Precision.HIGHEST


def layout(seq_lengths, seq_owner, bucket, capacity):
    owned = seq_owner == bucket
    owned_len = jnp.where(owned, seq_lengths, 0)
    order = jnp.arange(seq_lengths.shape[0], dtype=jnp.int32)
    starts = jnp.sum(jnp.where(order[None, :] < order[:, None], owned_len[None, :], 0), axis=1)
    places = jnp.arange(capacity, dtype=jnp.int32)[:, None]
    ends = starts + seq_lengths
    inside = owned[None, :] & (places >= starts[None, :]) & (places < ends[None, :])
    live_rows = jnp.any(inside, axis=1)
    seq_index = jnp.arange(seq_lengths.shape[0], dtype=jnp.int32)
    seq_ids = jnp.sum(jnp.where(inside, seq_index[None, :], 0), axis=1)
    seq_ids = jnp.where(live_rows, seq_ids, -1)
    return (seq_ids, live_rows.astype(jnp.float32))


def convolve(channels, kernel, offset, seq_ids, live_rows):
    tap_count = kernel.shape[0]
    summed_in = offset[None, :] + kernel[tap_count - 1][None, :] * channels
    for lag_steps in range(1, tap_count):
        lagged = jnp.concatenate(
            [jnp.zeros((lag_steps, channels.shape[1]), jnp.float32), channels[:-lag_steps]], axis=0
        )
        prior_ids = jnp.concatenate([jnp.full((lag_steps,), -1, jnp.int32), seq_ids[:-lag_steps]])
        same_seq = jnp.where((prior_ids == seq_ids) & (live_rows > 0), 1.0, 0.0).astype(jnp.float32)
        summed_in = (
            summed_in + kernel[tap_count - 1 - lag_steps][None, :] * lagged * same_seq[:, None]
        )
    return summed_in


def mix_bucket(values, bmat, cmat, sizes, rates, skip_gain, ids, live):
    rows_all, head_count, head_dim = values.shape
    lower = jnp.arange(rows_all)[:, None] >= jnp.arange(rows_all)[None, :]
    cumulated = jnp.dot(lower.astype(jnp.float32), rates, precision=PRECISE)
    pair_live = (
        (ids[:, None] == ids[None, :]) & (live[:, None] > 0) & (live[None, :] > 0) & lower
    )
    scores = jnp.dot(cmat, bmat.T, precision=PRECISE)
    gap = jnp.where(pair_live[:, :, None], cumulated[:, None, :] - cumulated[None, :, :], 0.0)
    weights = (
        jnp.exp(gap) * (pair_live.astype(jnp.float32) * scores)[:, :, None] * sizes[None, :, :]
    )
    within = jnp.einsum("tsh,shp->thp", weights, values, precision=PRECISE)
    mixed_out = (within + skip_gain[None, :, None] * values) * live[:, None, None]
    return mixed_out.reshape(rows_all, head_count * head_dim)


def sum_rows_over_dp(part, shared_cols=0):
    piece = lax.psum_scatter(
        part.astype(jnp.bfloat16), "dp", scatter_dimension=0, tiled=True
    )
    if shared_cols:
        own = piece.shape[1] - shared_cols
        tail = lax.psum(piece[:, own:].astype(jnp.float32), "col").astype(jnp.bfloat16)
        piece = jnp.concatenate([piece[:, :own], tail], axis=1)
    return lax.all_gather(piece, "dp", axis=0, tiled=True)


def mixer_local(
    conv_in,
    narrow_in,
    inner_kernel,
    inner_offset,
    shared_kernel,
    shared_offset,
    decay_log,
    step_bias,
    skip_gain,
    seq_ids,
    live_rows,
):
    inner_size = inner_kernel.shape[1]
    state_size = shared_kernel.shape[1] // 2
    head_count = decay_log.shape[0]
    shared_in = narrow_in[:, : 2 * state_size]
    step_raw = narrow_in[:, 2 * state_size :]
    mixed_x = jax.nn.silu(convolve(conv_in, inner_kernel, inner_offset, seq_ids, live_rows))
    mixed_bc = jax.nn.silu(convolve(shared_in, shared_kernel, shared_offset, seq_ids, live_rows))
    step_sizes = jax.nn.softplus(step_raw + step_bias[None, :])
    decay_rate = step_sizes * (-jnp.exp(decay_log))[None, :]
    values = mixed_x.reshape(mixed_x.shape[0], head_count, inner_size // head_count)
    return mix_bucket(
        values,
        mixed_bc[:, :state_size],
        mixed_bc[:, state_size:],
        step_sizes,
        decay_rate,
        skip_gain,
        seq_ids,
        live_rows,
    )


def per_device(
    block_input,
    cotangent,
    seq_lengths,
    seq_owner,
    norm_gain,
    proj_zx,
    proj_bc,
    proj_dt,
    proj_out,
    inner_kernel,
    inner_offset,
    shared_kernel,
    shared_offset,
    decay_log,
    step_bias,
    skip_gain,
    output_gain,
):
    row_count = lax.axis_size("row")
    col_count = lax.axis_size("col")
    row_index = lax.axis_index("row")
    col_index = lax.axis_index("col")
    data_index = lax.axis_index("dp")
    width_part = norm_gain.shape[0]
    inner_size = proj_zx.shape[2]
    state_size = proj_bc.shape[1] // 2
    tap_count = inner_kernel.shape[0]
    capacity = CAP
    bucket = data_index * row_count + row_index
    seq_ids, live_rows = layout(seq_lengths, seq_owner, bucket, capacity)
    rscale = lax.rsqrt(
        jnp.mean(jnp.square(block_input.astype(jnp.float32)), axis=1, keepdims=True) + EPSILON
    )
    own_cols = lax.dynamic_slice_in_dim(block_input, row_index * width_part, width_part, 1).astype(
        jnp.float32
    )
    normalized = own_cols * rscale
    gain_f = norm_gain.astype(jnp.float32)
    normed = (normalized * gain_f[None, :]).astype(jnp.bfloat16)
    normed_all = lax.all_gather(normed, "col", axis=0, tiled=True)
    weight_zx = proj_zx.reshape(width_part, 2 * inner_size)
    weight_narrow = jnp.concatenate([proj_bc, proj_dt], axis=1)
    zx_in = lax.psum_scatter(
        jnp.dot(normed_all, weight_zx, preferred_element_type=jnp.float32),
        "row",
        scatter_dimension=0,
        tiled=True,
    )
    narrow_in = lax.psum_scatter(
        jnp.dot(normed_all, weight_narrow, preferred_element_type=jnp.float32),
        "row",
        scatter_dimension=0,
        tiled=True,
    )
    gate_in = zx_in[:, :inner_size]
    conv_in = zx_in[:, inner_size:]

    def local_piece(*operands):
        return mixer_local(*operands, seq_ids, live_rows)

    ssm_rows, pull_back = jax.vjp(
        local_piece,
        conv_in,
        narrow_in,
        inner_kernel,
        inner_offset,
        shared_kernel,
        shared_offset,
        decay_log,
        step_bias,
        skip_gain,
    )
    gated_rows, gate_back = jax.vjp(
        lambda ssm_value, gate_value: ssm_value * jax.nn.silu(gate_value), ssm_rows, gate_in
    )
    square_sum = lax.psum(jnp.sum(gated_rows * gated_rows, axis=1), "col")
    rnorm = lax.rsqrt(square_sum / DI + EPSILON)[:, None]
    out_gain = output_gain.astype(jnp.float32)
    branch = (gated_rows * rnorm * out_gain[None, :]).astype(jnp.bfloat16)
    branch_all = lax.all_gather(branch, "row", axis=0, tiled=True)
    row_piece = branch_all
    branch_out = lax.psum_scatter(
        jnp.dot(row_piece, proj_out, preferred_element_type=jnp.float32),
        "col",
        scatter_dimension=0,
        tiled=True,
    )
    block_output = (own_cols + branch_out).astype(jnp.bfloat16)
    cot_all = lax.all_gather(cotangent, "col", axis=0, tiled=True)
    row_piece = cot_all
    branch_grad = lax.psum_scatter(
        lax.dot_general(
            row_piece, proj_out, (((1,), (1,)), ((), ())), preferred_element_type=jnp.float32
        ),
        "row",
        scatter_dimension=0,
        tiled=True,
    )
    outproj_part = lax.dot_general(
        branch_all, cot_all, (((0,), (0,)), ((), ())), preferred_element_type=jnp.float32
    )
    outproj_total = sum_rows_over_dp(outproj_part).astype(jnp.float32)
    scaled_grad = branch_grad * out_gain[None, :]
    cross_sum = lax.psum(jnp.sum(scaled_grad * gated_rows, axis=1), "col")
    gated_grad = rnorm * scaled_grad - gated_rows * rnorm**3 * (cross_sum / DI)[:, None]
    ogain_part = jnp.sum(branch_grad * gated_rows * rnorm, axis=0)
    ssm_grad, gate_grad = gate_back(gated_grad)
    gate_all = lax.all_gather(gate_grad.astype(jnp.bfloat16), "row", axis=0, tiled=True)
    gate_total = sum_rows_over_dp(
        lax.dot_general(
            normed_all, gate_all, (((0,), (0,)), ((), ())), preferred_element_type=jnp.float32
        )
    )
    local_grads = pull_back(ssm_grad)
    inner_all = lax.all_gather(
        local_grads[0].astype(jnp.bfloat16), "row", axis=0, tiled=True
    )
    narrow_all = lax.all_gather(
        local_grads[1].astype(jnp.bfloat16), "row", axis=0, tiled=True
    )
    normed_grad = lax.psum_scatter(
        lax.dot_general(
            jnp.concatenate([gate_all, inner_all], axis=1),
            weight_zx,
            (((1,), (1,)), ((), ())),
            preferred_element_type=jnp.float32,
        )
        + lax.dot_general(
            narrow_all, weight_narrow, (((1,), (1,)), ((), ())), preferred_element_type=jnp.float32
        ),
        "col",
        scatter_dimension=0,
        tiled=True,
    )
    inner_total = sum_rows_over_dp(
        lax.dot_general(
            normed_all, inner_all, (((0,), (0,)), ((), ())), preferred_element_type=jnp.float32
        )
    )
    narrow_part = lax.dot_general(
        normed_all, narrow_all, (((0,), (0,)), ((), ())), preferred_element_type=jnp.float32
    )
    narrow_total = sum_rows_over_dp(
        jnp.concatenate([narrow_part[:, 2 * state_size :], narrow_part[:, : 2 * state_size]], 1),
        2 * state_size,
    ).astype(jnp.float32)
    head_count = decay_log.shape[0]
    steps_total = narrow_total[:, :head_count]
    shared_total = narrow_total[:, head_count:]
    inproj_total = jnp.stack([gate_total, inner_total], axis=1).astype(jnp.float32)
    scaled_in = normed_grad * gain_f[None, :]
    norm_part = jnp.sum(normed_grad * normalized, axis=0)
    row_stat = lax.psum(jnp.sum(scaled_in * normalized, axis=1), "row")
    input_grad = cotangent.astype(jnp.float32) + rscale * (
        scaled_in - normalized * (row_stat / D)[:, None]
    )
    row_hot = (jnp.arange(row_count) == row_index).astype(jnp.float32)
    col_hot = (jnp.arange(col_count) == col_index).astype(jnp.float32)
    gain_slot = row_hot[:, None] * norm_part[None, :]
    head_stack = jnp.stack([local_grads[6], local_grads[7], local_grads[8]], axis=0)
    head_slot = col_hot[None, :, None] * head_stack[:, None, :]
    chan_stack = jnp.concatenate(
        [local_grads[2], local_grads[3][None, :], ogain_part[None, :]], axis=0
    )
    chan_slot = col_hot[None, :, None] * chan_stack[:, None, :]
    shared_stack = jnp.concatenate([local_grads[4], local_grads[5][None, :]], axis=0)
    slots = (gain_slot, head_slot, chan_slot, shared_stack)
    flat = lax.psum(
        jnp.concatenate([slot.reshape(-1) for slot in slots]), ("dp", "row", "col")
    )
    summed, place = [], 0
    for slot in slots:
        summed.append(flat[place : place + slot.size].reshape(slot.shape))
        place += slot.size
    gain_total = lax.dynamic_index_in_dim(summed[0], row_index, 0, keepdims=False)
    head_total = lax.dynamic_index_in_dim(summed[1], col_index, 1, keepdims=False)
    chan_total = lax.dynamic_index_in_dim(summed[2], col_index, 1, keepdims=False)
    stack_total = summed[3]
    return (
        block_output,
        input_grad,
        gain_total,
        inproj_total,
        shared_total,
        steps_total,
        outproj_total,
        chan_total[:tap_count],
        chan_total[tap_count],
        stack_total[:tap_count],
        stack_total[tap_count],
        head_total[0],
        head_total[1],
        head_total[2],
        chan_total[tap_count + 1],
    )


def solution(mesh):
    return jax.shard_map(
        per_device,
        mesh=mesh,
        in_specs=(
            P(("dp", "col"), None),
            P(("dp", "col"), "row"),
            P(),
            P(),
            P("row"),
            P("row", None, "col"),
            P("row", None),
            P("row", "col"),
            P("col", "row"),
            P(None, "col"),
            P("col"),
            P(),
            P(),
            P("col"),
            P("col"),
            P("col"),
            P("col"),
        ),
        out_specs=(
            P(("dp", "col"), "row"),
            P(("dp", "col"), "row"),
            P("row"),
            P("row", None, "col"),
            P("row", None),
            P("row", "col"),
            P("col", "row"),
            P(None, "col"),
            P("col"),
            P(),
            P(),
            P("col"),
            P("col"),
            P("col"),
            P("col"),
        ),
        check_vma=False,
    )
```
